32 devices in a mesh: row: 4 (over y, core), col: 8 (over z, x).
Axes of the slice: x: 2, y: 2, z: 4, core: 2. Of those that a mesh axis runs over, the one named last changes fastest.
Arguments:
- a_blocks: float32 [512, 128, 128], P(('row', 'col')), may hold values from -0.5 to 0.5
- a_index: int32 [512], replicated, may hold values from -1 to 31, as said below
- p_blocks: float32 [256, 128, 128], P(('row', 'col')), may hold values from -6 to 6
- p_index: int32 [256], replicated, may hold values from -1 to 31, as said below
- owners: int32 [4], replicated, may hold values from 0 to 7, as said below
Outputs:
- coarse: float32 [4096, 4096], P('row', 'col')
The draws below stay inside these ranges and needn't reach their ends.
Inputs may be any that keep to these rules, and one draw needn't show every extreme that they name: `a_index`: live entries (not -1) of one grid position's 16 slots are distinct and stand before its empty slots; some position has all 16 slots live. `p_index`: live entries (not -1) of one grid position's 8 slots are distinct and stand before its empty slots; some position has all 8 slots live. `owners`: the 4 panels are distinct.
All inputs are finite; a program needn't handle non-finite values.
Results may differ from the reference program's by a relative error of at most 0.0003.
Values sent between devices are 32-bit elements; how exact they have to be, the bound alone decides.
A program may use at most 128 MiB of HBM per device.

```python
import jax
import jax.numpy as jnp
from jax import lax

BLOCK = 128
ROW_BLOCKS = 8
COL_BLOCKS = 4
STEPS = 4
PANEL = 4
INNER_ROWS = 8
A_SLOTS = 16
P_SLOTS = 8
A_ALL = 512
P_ALL = 256
ROWS = 4096
COLS = 4096
N_ROW = 4
N_COL = 8


def slot_pattern(key, slot_count, positions):
    devices = N_ROW * N_COL

    def one_device(device_key):
        return jax.random.permutation(device_key, positions)[:slot_count].astype(jnp.int32)
    device_keys = jax.random.split(jax.random.fold_in(key, 11), devices)
    chosen = jax.vmap(one_device)(device_keys)
    lowest = max(slot_count // 8, 1)
    first = jax.random.randint(jax.random.fold_in(key, 12), (devices,), lowest, slot_count + 1)
    second = jax.random.randint(jax.random.fold_in(key, 13), (devices,), lowest, slot_count + 1)
    live_count = jnp.minimum(first, second)
    fullest = jax.random.randint(jax.random.fold_in(key, 14), (), 0, devices)
    device_number = jnp.arange(devices)
    live_count = jnp.where(device_number == (fullest + 1) % devices, lowest, live_count)
    live_count = jnp.where(device_number == fullest, slot_count, live_count)
    slot_rank = jnp.arange(slot_count)[None, :]
    pattern = jnp.where(slot_rank < live_count[:, None], chosen, -1)
    return pattern.reshape(devices * slot_count).astype(jnp.int32)


def draw_a_index(key, part):
    return slot_pattern(jax.random.fold_in(key, 3), A_SLOTS, ROW_BLOCKS * PANEL)


def draw_p_index(key, part):
    return slot_pattern(jax.random.fold_in(key, 5), P_SLOTS, INNER_ROWS * COL_BLOCKS)


def draw_owners(key, part):
    middle = jax.random.permutation(jax.random.fold_in(key, 21), N_COL - 2)[:STEPS - 2] + 1
    listed = jnp.concatenate([jnp.array([0, N_COL - 1], jnp.int32), middle.astype(jnp.int32)])
    shuffle = jax.random.permutation(jax.random.fold_in(key, 22), STEPS)
    return listed[shuffle].astype(jnp.int32)


def steps_of(rng, dims, cuts, least, top_value):
    loudness, own = 1.0, jax.random.fold_in(rng, 6)
    for dim, parts in cuts:
        steps = jnp.exp(jax.random.uniform(jax.random.fold_in(own, dim), (parts,), jnp.float32, least / len(cuts), top_value / len(cuts)))
        loudness = loudness * jnp.repeat(steps, dims[dim] // parts).reshape([-1 if axis == dim else 1 for axis in range(len(dims))])
    return loudness


def centred(own_key, shape, width, reach, cuts=(), kind=jnp.bfloat16):
    result = jax.random.normal(own_key, shape, jnp.float32) * width
    if len(cuts) > 0:
        result = steps_of(own_key, shape, cuts, -0.22, 0.18) * result
    return jnp.clip(result, min=-reach, max=reach).astype(kind)


def setup_inputs(seed: int = 0) -> dict:
    keys = jax.random.split(jax.random.key(seed), 6)
    return {
        "a_blocks": centred(keys[0], (A_ALL, BLOCK, BLOCK), BLOCK ** -0.5, 0.5, ((0, 32),), jnp.float32),
        "a_index": draw_a_index(jax.random.fold_in(keys[5], 71), 0),
        "p_blocks": centred(keys[2], (P_ALL, BLOCK, BLOCK), 1.0, 6.0, ((0, 32),), jnp.float32),
        "p_index": draw_p_index(jax.random.fold_in(keys[5], 71), 0),
        "owners": draw_owners(jax.random.fold_in(keys[5], 71), 0),
    }


precise = lax.Precision.HIGHEST


def reference(a_blocks, a_index, p_blocks, p_index, owners):
    a_grid = a_blocks.reshape(N_ROW, N_COL, A_SLOTS, BLOCK, BLOCK)
    a_places = a_index.reshape(N_ROW, N_COL, A_SLOTS)
    p_grid = p_blocks.reshape(N_ROW, N_COL, P_SLOTS, BLOCK, BLOCK)
    p_places = p_index.reshape(N_ROW, N_COL, P_SLOTS)
    panels = []
    for step_number in range(STEPS):
        owner = owners[step_number]
        holder = owner * N_ROW // N_COL
        offset = owner * PANEL - holder * INNER_ROWS
        held_index = p_places[holder]
        held_blocks = p_grid[holder]
        live_mask = held_index >= 0
        inner_place = held_index // COL_BLOCKS - offset
        column_place = held_index % COL_BLOCKS
        pick_inner = ((inner_place[:, :, None] == jnp.arange(PANEL, dtype=jnp.int32)[None, None, :])
                      & live_mask[:, :, None]).astype(jnp.float32)
        pick_column = (column_place[:, :, None] == jnp.arange(COL_BLOCKS, dtype=jnp.int32)[None, None, :]).astype(jnp.float32)
        spread = jnp.einsum('csk,csj,csab->kacjb', pick_inner, pick_column, held_blocks, precision=precise)
        panels.append(spread.reshape(PANEL, BLOCK, COLS))

    def one_row(row_number):
        running = jnp.zeros((ROW_BLOCKS, BLOCK, COLS), jnp.float32)
        for step_number in range(STEPS):
            owner = owners[step_number]
            blocks = a_grid[row_number, owner]
            placing = a_places[row_number, owner]
            live_mask = placing >= 0
            row_place = placing // PANEL
            inner_place = placing % PANEL
            chosen = panels[step_number][inner_place]
            masked = blocks * live_mask[:, None, None].astype(blocks.dtype)
            products = jnp.einsum('sab,sbn->san', masked, chosen, precision=precise)
            pick_row = ((row_place[None, :] == jnp.arange(ROW_BLOCKS, dtype=jnp.int32)[:, None])
                        & live_mask[None, :]).astype(jnp.float32)
            running = running + jnp.einsum('rs,san->ran', pick_row, products, precision=precise)
        return running.reshape(ROW_BLOCKS * BLOCK, COLS)

    stacked = lax.map(one_row, jnp.arange(N_ROW, dtype=jnp.int32))
    return stacked.reshape(ROWS, COLS)
```

```python
import functools

import jax
import jax.numpy as jnp
from jax import lax
from jax.experimental import pallas as pl
from jax.experimental.pallas import tpu as pltpu
from jax.sharding import PartitionSpec as P

ROW_BLOCKS = 8
COL_BLOCKS = 4
STEPS = 4
LAG = 2
LIMITS = (24, 32, 40, 48, 64)
MESH = pl.DeviceIdType.MESH


def pick(flag, yes, no):
    return lax.select_n(flag, no, yes)


def gather_kernel(
    nz, nx, rows, length,
    offs, owners, a_ref, p_ref,
    a_all, p_all,
    xin_out, xin, src, up, down,
    xin_s, xin_r, up_s, up_r, dn_s, dn_r, xo_s, xo_r, p_s, p_r, own_s,
):
    col = lax.axis_index("col")
    row = lax.axis_index("row")
    z, x = col // nx, col % nx
    slots = a_ref.shape[0]
    share = slots // nx

    barrier = pltpu.get_barrier_semaphore()
    for dz in (1, nz - 1):
        pl.semaphore_signal(
            barrier, inc=1, device_id={"col": (z + dz) % nz * nx + x}, device_id_type=MESH
        )
    for d in range(1, nx):
        pl.semaphore_signal(
            barrier, inc=1, device_id={"col": z * nx + (x + d) % nx}, device_id_type=MESH
        )
    for d in range(1, rows):
        pl.semaphore_signal(barrier, inc=1, device_id={"row": (row + d) % rows}, device_id_type=MESH)
    pl.semaphore_wait(barrier, 2 + nx - 1 + rows - 1)

    def remote(source, target, send, recv, device):
        return pltpu.make_async_remote_copy(
            src_ref=source, dst_ref=target, send_sem=send, recv_sem=recv,
            device_id=device, device_id_type=MESH,
        )

    def xin_copy(d, k):
        return remote(
            xin_out.at[d - 1, k], xin.at[d - 1, k], xin_s.at[d - 1, k], xin_r.at[d - 1, k],
            {"col": z * nx + (x + d) % nx},
        )

    def up_copy(q):
        return remote(
            up.at[q], up.at[q], up_s.at[q], up_r.at[q], {"col": (z + 1) % nz * nx + x}
        )

    def down_copy(q):
        return remote(
            down.at[q], down.at[q], dn_s.at[q], dn_r.at[q], {"col": (z + nz - 1) % nz * nx + x}
        )

    def xo_copy(d, q, line):
        rank = q * nx + line
        return remote(
            a_all.at[rank], a_all.at[rank], xo_s.at[d - 1, q], xo_r.at[d - 1, q],
            {"col": z * nx + (x + d) % nx},
        )

    def p_copy(d, origin):
        return remote(
            p_ref, p_all.at[origin], p_s.at[d - 1], p_r.at[d - 1], {"row": (row + d) % rows}
        )

    own_p = pltpu.make_async_copy(p_ref, p_all.at[row], own_s)

    starts = [offs[t] for t in range(STEPS)]
    held = [owners[t] for t in range(STEPS)]
    my_start = jnp.int32(0)
    for t in range(STEPS):
        my_start = my_start + jnp.where(held[t] == col, starts[t], 0)

    def rank_info(rank):
        owner, first = held[0], starts[0]
        for t in range(1, STEPS):
            later = rank >= starts[t]
            owner = jnp.where(later, held[t], owner)
            first = jnp.where(later, starts[t], first)
        return owner, jnp.clip(rank - first, 0, slots - 1)

    for k in range(share):
        for d in range(1, nx):
            part = lax.rem((x + d) % nx + slots * STEPS * nx - my_start, nx)
            xin_out[d - 1, k] = a_ref[k * nx + part]
            xin_copy(d, k).start()
    for d in range(1, rows):
        p_copy(d, row).start()
    own_p.start()

    up_lag = z * LAG
    down_lag = (nz - 1 - z) * LAG
    last_lag = jnp.maximum(up_lag, down_lag)

    def step(n, carry):
        @pl.when(n < length)
        def _():
            @pl.when(n < share)
            def _():
                for d in range(1, nx):
                    xin_copy(d, n).wait_recv()

            owner, slot = rank_info(n * nx + x)
            apart = lax.rem(x + nx - owner % nx, nx)
            place = slot // nx
            value = a_ref[slot]
            for d in range(1, nx):
                def choose(k, kept, d=d):
                    return pick((apart == d) & (place == k), xin[d - 1, k], kept)

                value = lax.fori_loop(0, jnp.minimum(n + 1, share), choose, value)
            src[n] = value

        q_up = n - up_lag

        @pl.when((q_up >= 0) & (q_up < length))
        def _():
            @pl.when(z == 0)
            def _():
                up[q_up] = src[q_up]

            @pl.when(z > 0)
            def _():
                up_copy(q_up).wait_recv()
                owner, _ = rank_info(q_up * nx + x)
                up[q_up] = pick(owner // nx == z, src[q_up], up[q_up])

            @pl.when(z < nz - 1)
            def _():
                up_copy(q_up).start()

        q_down = n - down_lag

        @pl.when((q_down >= 0) & (q_down < length))
        def _():
            @pl.when(z == nz - 1)
            def _():
                down[q_down] = src[q_down]

            @pl.when(z < nz - 1)
            def _():
                down_copy(q_down).wait_recv()
                owner, _ = rank_info(q_down * nx + x)
                down[q_down] = pick(owner // nx == z, src[q_down], down[q_down])

            @pl.when(z > 0)
            def _():
                down_copy(q_down).start()

        q = n - last_lag

        @pl.when((q >= 0) & (q < length))
        def _():
            owner, _ = rank_info(q * nx + x)
            a_all[q * nx + x] = pick(owner // nx <= z, up[q], down[q])
            for d in range(1, nx):
                xo_copy(d, q, x).start()

        return carry

    lax.fori_loop(0, length + (nz - 1) * LAG, step, 0)

    def finish(q, carry):
        @pl.when(z < nz - 1)
        def _():
            up_copy(q).wait_send()

        @pl.when(z > 0)
        def _():
            down_copy(q).wait_send()

        for d in range(1, nx):
            @pl.when(q < share)
            def _(d=d):
                xin_copy(d, q).wait_send()

            xo_copy(d, q, x).wait_send()
            xo_copy(d, q, (x + nx - d) % nx).wait_recv()
        return carry

    lax.fori_loop(0, length, finish, 0)
    for k in range(length, share):
        for d in range(1, nx):
            xin_copy(d, k).wait_send()
            xin_copy(d, k).wait_recv()
    for d in range(1, rows):
        p_copy(d, row).wait_send()
        p_copy(d, (row + rows - d) % rows).wait_recv()
    own_p.wait()


def gather_live(nz, nx, rows, limit, number, offs, owners, a_blocks, p_blocks):
    slots, block = a_blocks.shape[0], a_blocks.shape[1]
    length = limit // nx
    share = slots // nx
    tile = (block, block)
    dma = pltpu.SemaphoreType.DMA
    return pl.pallas_call(
        functools.partial(gather_kernel, nz, nx, rows, length),
        out_shape=(
            jax.ShapeDtypeStruct((limit,) + tile, jnp.float32),
            jax.ShapeDtypeStruct((rows,) + p_blocks.shape, jnp.float32),
        ),
        in_specs=[
            pl.BlockSpec(memory_space=pltpu.SMEM),
            pl.BlockSpec(memory_space=pltpu.SMEM),
            pl.BlockSpec(memory_space=pltpu.VMEM),
            pl.BlockSpec(memory_space=pl.ANY),
        ],
        out_specs=(
            pl.BlockSpec(memory_space=pltpu.VMEM),
            pl.BlockSpec(memory_space=pl.ANY),
        ),
        scratch_shapes=[
            pltpu.VMEM((nx - 1, share) + tile, jnp.float32),
            pltpu.VMEM((nx - 1, share) + tile, jnp.float32),
            pltpu.VMEM((length,) + tile, jnp.float32),
            pltpu.VMEM((length,) + tile, jnp.float32),
            pltpu.VMEM((length,) + tile, jnp.float32),
            dma((nx - 1, share)), dma((nx - 1, share)),
            dma((length,)), dma((length,)),
            dma((length,)), dma((length,)),
            dma((nx - 1, length)), dma((nx - 1, length)),
            dma((rows - 1,)), dma((rows - 1,)),
            dma,
        ],
        compiler_params=pltpu.CompilerParams(
            collective_id=number, has_side_effects=True, vmem_limit_bytes=40 * 1024 * 1024
        ),
    )(offs, owners, a_blocks, p_blocks)


def split(value):
    high = value.astype(jnp.bfloat16)
    return high, (value - high.astype(jnp.float32)).astype(jnp.bfloat16)


def product_kernel(
    rows, cols, a_slots, width, offs, owners, a_index, p_index, a_all, p_all, out, table
):
    block = a_all.shape[1]
    p_slots = p_all.shape[1]
    row, col = lax.axis_index("row"), lax.axis_index("col")
    out[...] = jnp.zeros_like(out)
    span = width * COL_BLOCKS

    def clear(n, carry):
        table[n] = -1
        return carry

    lax.fori_loop(0, STEPS * span, clear, 0)
    for t in range(STEPS):
        owner = owners[t]
        holder = owner * rows // cols
        offset = owner * width - holder * ROW_BLOCKS
        first = offs[t]
        base = (row * cols + owner) * a_slots

        def place(s, carry):
            entry = p_index[(holder * cols + col) * p_slots + s]
            inner = entry // COL_BLOCKS - offset

            @pl.when((entry >= 0) & (inner >= 0) & (inner < width))
            def _():
                table[t * span + inner * COL_BLOCKS + entry % COL_BLOCKS] = s

            return carry

        lax.fori_loop(0, p_slots, place, 0)

        def one(s, carry):
            entry = a_index[base + s]
            down_rows = entry // width
            inner = entry % width
            for c in range(COL_BLOCKS):
                slot = table[t * span + inner * COL_BLOCKS + c]

                @pl.when(slot >= 0)
                def _():
                    left_high, left_low = split(a_all[first + s])
                    right_high, right_low = split(p_all[holder, slot])
                    dot = functools.partial(jnp.dot, preferred_element_type=jnp.float32)
                    value = dot(left_high, right_high) + (
                        dot(left_high, right_low) + dot(left_low, right_high)
                    )
                    where = pl.ds(pl.multiple_of(down_rows * block, block), block)
                    out[where, c * block : (c + 1) * block] += value

            return carry

        lax.fori_loop(0, offs[t + 1] - first, one, 0)


def multiply(rows, cols, a_slots, offs, owners, a_index, p_index, a_all, p_all):
    block = a_all.shape[1]
    width = ROW_BLOCKS * rows // cols
    smem = pl.BlockSpec(memory_space=pltpu.SMEM)
    vmem = pl.BlockSpec(memory_space=pltpu.VMEM)
    return pl.pallas_call(
        functools.partial(product_kernel, rows, cols, a_slots, width),
        out_shape=jax.ShapeDtypeStruct((ROW_BLOCKS * block, COL_BLOCKS * block), jnp.float32),
        in_specs=[smem, smem, smem, smem, vmem, vmem],
        out_specs=vmem,
        scratch_shapes=[pltpu.SMEM((STEPS * width * COL_BLOCKS,), jnp.int32)],
        compiler_params=pltpu.CompilerParams(vmem_limit_bytes=40 * 1024 * 1024),
    )(offs, owners, a_index, p_index, a_all, p_all)


def local(a_blocks, a_index, p_blocks, p_index, owners):
    cols = lax.axis_size("col")
    rows = lax.axis_size("row")
    nz = 4
    nx = cols // nz
    slots = a_blocks.shape[0]
    counts = jnp.sum((a_index.reshape(rows, cols, slots) >= 0).astype(jnp.int32), axis=2)
    chosen = (owners[:, None] == jnp.arange(cols, dtype=jnp.int32)[None, :]).astype(jnp.int32)
    picked = jnp.sum(counts[:, None, :] * chosen[None, :, :], axis=2)
    before = (jnp.arange(STEPS)[None, :] < jnp.arange(STEPS + 1)[:, None]).astype(jnp.int32)
    sums = jnp.sum(picked[:, None, :] * before[None, :, :], axis=2)
    most = jnp.max(sums[:, STEPS])
    offs = lax.dynamic_index_in_dim(sums, lax.axis_index("row"), 0, keepdims=False)
    branch = jnp.int32(0)
    for limit in LIMITS[:-1]:
        branch = branch + (most > limit).astype(jnp.int32)

    def make(number, limit):
        def run(offs, owners, a_blocks, a_index, p_blocks, p_index):
            a_all, p_all = gather_live(
                nz, nx, rows, limit, number, offs, owners, a_blocks, p_blocks
            )
            return multiply(rows, cols, slots, offs, owners, a_index, p_index, a_all, p_all)

        return run

    branches = [make(number, limit) for number, limit in enumerate(LIMITS)]
    return lax.switch(branch, branches, offs, owners, a_blocks, a_index, p_blocks, p_index)


def solution(mesh):
    in_specs = (P(("row", "col"), None, None), P(), P(("row", "col"), None, None), P(), P())
    out_specs = P("row", "col")
    return jax.shard_map(local, mesh=mesh, in_specs=in_specs, out_specs=out_specs, check_vma=False)
```

```python
import functools

import jax
import jax.numpy as jnp
from jax import lax
from jax.experimental import pallas as pl
from jax.experimental.pallas import tpu as pltpu
from jax.sharding import PartitionSpec as P

ROW_BLOCKS = 8
COL_BLOCKS = 4
STEPS = 4
LAG = 2
LIMITS = (16, 19, 22, 25, 28, 32, 40, 64)
MESH = pl.DeviceIdType.MESH


def pick(flag, yes, no):
    return lax.select_n(flag, no, yes)


def plan_kernel(rows, cols, nx, slots, a_index, owners, plan):
    row = lax.axis_index("row")
    held = [owners[t] for t in range(STEPS)]
    lines = [held[t] % nx for t in range(STEPS)]

    def one(i, longest):
        starts, counts = [], []
        for t in range(STEPS):
            base = (i * cols + held[t]) * slots
            count = jnp.int32(0)
            width = slots // 2
            while width:
                count = count + jnp.where(a_index[base + count + width - 1] >= 0, width, 0)
                width //= 2
            count = count + jnp.where(a_index[base + count] >= 0, 1, 0)
            start = jnp.int32(0)
            for e in range(t):
                start = start + jnp.where(lines[e] == lines[t], counts[e], 0)
            starts.append(start)
            counts.append(count)
            longest = jnp.maximum(longest, start + count)

        @pl.when(i == row)
        def _():
            for t in range(STEPS):
                plan[t] = starts[t]
                plan[STEPS + t] = counts[t]

        return longest

    longest = jnp.int32(0)
    for i in range(rows):
        longest = one(i, longest)
    branch = jnp.int32(0)
    for limit in LIMITS[:-1]:
        branch = branch + jnp.where(longest > limit, 1, 0)
    plan[2 * STEPS] = branch


def make_plan(rows, cols, nx, slots, a_index, owners):
    smem = pl.BlockSpec(memory_space=pltpu.SMEM)
    return pl.pallas_call(
        functools.partial(plan_kernel, rows, cols, nx, slots),
        out_shape=jax.ShapeDtypeStruct((2 * STEPS + 1,), jnp.int32),
        in_specs=[smem, smem],
        out_specs=smem,
    )(a_index, owners)


def gather_kernel(
    nz, nx, rows, length,
    plan, owners, a_ref, p_ref,
    a_all, p_all,
    up, down,
    up_s, up_r, dn_s, dn_r, xo_s, xo_r, p_s, p_r, own_s,
):
    col = lax.axis_index("col")
    row = lax.axis_index("row")
    z, x = col // nx, col % nx
    slots = a_ref.shape[0]

    barrier = pltpu.get_barrier_semaphore()
    for dz in (1, nz - 1):
        pl.semaphore_signal(
            barrier, inc=1, device_id={"col": (z + dz) % nz * nx + x}, device_id_type=MESH
        )
    for d in range(1, nx):
        pl.semaphore_signal(
            barrier, inc=1, device_id={"col": z * nx + (x + d) % nx}, device_id_type=MESH
        )
    for d in range(1, rows):
        pl.semaphore_signal(barrier, inc=1, device_id={"row": (row + d) % rows}, device_id_type=MESH)
    pl.semaphore_wait(barrier, 2 + nx - 1 + rows - 1)

    def remote(source, target, send, recv, device):
        return pltpu.make_async_remote_copy(
            src_ref=source, dst_ref=target, send_sem=send, recv_sem=recv,
            device_id=device, device_id_type=MESH,
        )

    def up_copy(q):
        return remote(
            up.at[q], up.at[q], up_s.at[q], up_r.at[q], {"col": (z + 1) % nz * nx + x}
        )

    def down_copy(q):
        return remote(
            down.at[q], down.at[q], dn_s.at[q], dn_r.at[q], {"col": (z + nz - 1) % nz * nx + x}
        )

    def xo_copy(d, q, line):
        place = q * nx + line
        return remote(
            a_all.at[place], a_all.at[place], xo_s.at[d - 1, q], xo_r.at[d - 1, q],
            {"col": z * nx + (x + d) % nx},
        )

    def p_copy(d, origin):
        return remote(
            p_ref, p_all.at[origin], p_s.at[d - 1], p_r.at[d - 1], {"row": (row + d) % rows}
        )

    own_p = pltpu.make_async_copy(p_ref, p_all.at[row], own_s)
    starts = [plan[t] for t in range(STEPS)]
    held = [owners[t] for t in range(STEPS)]

    def holder_of(q):
        level, first = jnp.int32(0), jnp.int32(0)
        for t in range(STEPS):
            later = (held[t] % nx == x) & (q >= starts[t])
            level = jnp.where(later, held[t] // nx, level)
            first = jnp.where(later, starts[t], first)
        return level, jnp.clip(q - first, 0, slots - 1)

    for d in range(1, rows):
        p_copy(d, row).start()
    own_p.start()

    up_lag = z * LAG
    down_lag = (nz - 1 - z) * LAG
    last_lag = jnp.maximum(up_lag, down_lag)

    def step(n, carry):
        q_up = n - up_lag

        @pl.when((q_up >= 0) & (q_up < length))
        def _():
            level, slot = holder_of(q_up)

            @pl.when(z == 0)
            def _():
                up[q_up] = a_ref[slot]

            @pl.when(z > 0)
            def _():
                up_copy(q_up).wait_recv()
                up[q_up] = pick(level == z, a_ref[slot], up[q_up])

            @pl.when(z < nz - 1)
            def _():
                up_copy(q_up).start()

        q_down = n - down_lag

        @pl.when((q_down >= 0) & (q_down < length))
        def _():
            level, slot = holder_of(q_down)

            @pl.when(z == nz - 1)
            def _():
                down[q_down] = a_ref[slot]

            @pl.when(z < nz - 1)
            def _():
                down_copy(q_down).wait_recv()
                down[q_down] = pick(level == z, a_ref[slot], down[q_down])

            @pl.when(z > 0)
            def _():
                down_copy(q_down).start()

        q = n - last_lag

        @pl.when((q >= 0) & (q < length))
        def _():
            level, _ = holder_of(q)
            a_all[q * nx + x] = pick(level <= z, up[q], down[q])
            for d in range(1, nx):
                xo_copy(d, q, x).start()

        return carry

    lax.fori_loop(0, length + (nz - 1) * LAG, step, 0)

    def finish(q, carry):
        @pl.when(z < nz - 1)
        def _():
            up_copy(q).wait_send()

        @pl.when(z > 0)
        def _():
            down_copy(q).wait_send()

        for d in range(1, nx):
            xo_copy(d, q, x).wait_send()
            xo_copy(d, q, (x + nx - d) % nx).wait_recv()
        return carry

    lax.fori_loop(0, length, finish, 0)
    for d in range(1, rows):
        p_copy(d, row).wait_send()
        p_copy(d, (row + rows - d) % rows).wait_recv()
    own_p.wait()


def gather_live(nz, nx, rows, length, number, plan, owners, a_blocks, p_blocks):
    block = a_blocks.shape[1]
    tile = (block, block)
    dma = pltpu.SemaphoreType.DMA
    return pl.pallas_call(
        functools.partial(gather_kernel, nz, nx, rows, length),
        out_shape=(
            jax.ShapeDtypeStruct((length * nx,) + tile, jnp.float32),
            jax.ShapeDtypeStruct((rows,) + p_blocks.shape, jnp.float32),
        ),
        in_specs=[
            pl.BlockSpec(memory_space=pltpu.SMEM),
            pl.BlockSpec(memory_space=pltpu.SMEM),
            pl.BlockSpec(memory_space=pltpu.VMEM),
            pl.BlockSpec(memory_space=pl.ANY),
        ],
        out_specs=(
            pl.BlockSpec(memory_space=pltpu.VMEM),
            pl.BlockSpec(memory_space=pl.ANY),
        ),
        scratch_shapes=[
            pltpu.VMEM((length,) + tile, jnp.float32),
            pltpu.VMEM((length,) + tile, jnp.float32),
            dma((length,)), dma((length,)),
            dma((length,)), dma((length,)),
            dma((nx - 1, length)), dma((nx - 1, length)),
            dma((rows - 1,)), dma((rows - 1,)),
            dma,
        ],
        compiler_params=pltpu.CompilerParams(
            collective_id=number, has_side_effects=True, vmem_limit_bytes=40 * 1024 * 1024
        ),
    )(plan, owners, a_blocks, p_blocks)


def split(value):
    high = value.astype(jnp.bfloat16)
    return high, (value - high.astype(jnp.float32)).astype(jnp.bfloat16)


def product_kernel(
    rows, cols, nx, a_slots, width, plan, owners, a_index, p_index, a_all, p_all, out, table
):
    block = a_all.shape[1]
    p_slots = p_all.shape[1]
    row, col = lax.axis_index("row"), lax.axis_index("col")
    out[...] = jnp.zeros_like(out)
    span = width * COL_BLOCKS

    def clear(n, carry):
        table[n] = -1
        return carry

    lax.fori_loop(0, STEPS * span, clear, 0)
    for t in range(STEPS):
        owner = owners[t]
        holder = owner * rows // cols
        offset = owner * width - holder * ROW_BLOCKS
        first = plan[t]
        line = owner % nx
        base = (row * cols + owner) * a_slots

        def place(s, carry):
            entry = p_index[(holder * cols + col) * p_slots + s]
            inner = entry // COL_BLOCKS - offset

            @pl.when((entry >= 0) & (inner >= 0) & (inner < width))
            def _():
                table[t * span + inner * COL_BLOCKS + entry % COL_BLOCKS] = s

            return carry

        lax.fori_loop(0, p_slots, place, 0)

        def one(s, carry):
            entry = a_index[base + s]
            down_rows = entry // width
            inner = entry % width
            for c in range(COL_BLOCKS):
                slot = table[t * span + inner * COL_BLOCKS + c]

                @pl.when(slot >= 0)
                def _():
                    left_high, left_low = split(a_all[(first + s) * nx + line])
                    right_high, right_low = split(p_all[holder, slot])
                    dot = functools.partial(jnp.dot, preferred_element_type=jnp.float32)
                    value = dot(left_high, right_high) + (
                        dot(left_high, right_low) + dot(left_low, right_high)
                    )
                    where = pl.ds(pl.multiple_of(down_rows * block, block), block)
                    out[where, c * block : (c + 1) * block] += value

            return carry

        lax.fori_loop(0, plan[STEPS + t], one, 0)


def multiply(rows, cols, nx, a_slots, plan, owners, a_index, p_index, a_all, p_all):
    block = a_all.shape[1]
    width = ROW_BLOCKS * rows // cols
    smem = pl.BlockSpec(memory_space=pltpu.SMEM)
    vmem = pl.BlockSpec(memory_space=pltpu.VMEM)
    return pl.pallas_call(
        functools.partial(product_kernel, rows, cols, nx, a_slots, width),
        out_shape=jax.ShapeDtypeStruct((ROW_BLOCKS * block, COL_BLOCKS * block), jnp.float32),
        in_specs=[smem, smem, smem, smem, vmem, vmem],
        out_specs=vmem,
        scratch_shapes=[pltpu.SMEM((STEPS * width * COL_BLOCKS,), jnp.int32)],
        compiler_params=pltpu.CompilerParams(vmem_limit_bytes=40 * 1024 * 1024),
    )(plan, owners, a_index, p_index, a_all, p_all)


def local(a_blocks, a_index, p_blocks, p_index, owners):
    cols = lax.axis_size("col")
    rows = lax.axis_size("row")
    nz = 4
    nx = cols // nz
    slots = a_blocks.shape[0]
    plan = make_plan(rows, cols, nx, slots, a_index, owners)

    def make(number, length):
        def run(plan, owners, a_blocks, a_index, p_blocks, p_index):
            a_all, p_all = gather_live(
                nz, nx, rows, length, number, plan, owners, a_blocks, p_blocks
            )
            return multiply(rows, cols, nx, slots, plan, owners, a_index, p_index, a_all, p_all)

        return run

    branches = [make(number, length) for number, length in enumerate(LIMITS)]
    return lax.switch(
        plan[2 * STEPS], branches, plan, owners, a_blocks, a_index, p_blocks, p_index
    )


def solution(mesh):
    in_specs = (P(("row", "col"), None, None), P(), P(("row", "col"), None, None), P(), P())
    out_specs = P("row", "col")
    return jax.shard_map(local, mesh=mesh, in_specs=in_specs, out_specs=out_specs, check_vma=False)
```

```python
import functools

import jax
import jax.numpy as jnp
from jax import lax
from jax.experimental import pallas as pl
from jax.experimental.pallas import tpu as pltpu
from jax.sharding import PartitionSpec as P

ROW_BLOCKS = 8
COL_BLOCKS = 4
STEPS = 4
LAG = 5
LIMITS = (22, 26, 29, 32, 35, 38, 42, 48, 64)
MESH = pl.DeviceIdType.MESH


def pick(flag, yes, no):
    return lax.select_n(flag, no, yes)


def plan_kernel(rows, cols, slots, a_index, owners, plan):
    row = lax.axis_index("row")
    held = [owners[t] for t in range(STEPS)]

    def one(i, longest):
        starts, counts = [], []
        for t in range(STEPS):
            base = (i * cols + held[t]) * slots
            count = jnp.int32(0)
            width = slots // 2
            while width:
                count = count + jnp.where(a_index[base + count + width - 1] >= 0, width, 0)
                width //= 2
            count = count + jnp.where(a_index[base + count] >= 0, 1, 0)
            start = jnp.int32(0)
            for e in range(t):
                start = start + counts[e]
            starts.append(start)
            counts.append(count)
            longest = jnp.maximum(longest, start + count)

        @pl.when(i == row)
        def _():
            for t in range(STEPS):
                plan[t] = starts[t]
                plan[STEPS + t] = counts[t]

        return longest

    longest = jnp.int32(0)
    for i in range(rows):
        longest = one(i, longest)
    branch = jnp.int32(0)
    for limit in LIMITS[:-1]:
        branch = branch + jnp.where(longest > limit, 1, 0)
    plan[2 * STEPS] = branch


def make_plan(rows, cols, slots, a_index, owners):
    smem = pl.BlockSpec(memory_space=pltpu.SMEM)
    return pl.pallas_call(
        functools.partial(plan_kernel, rows, cols, slots),
        out_shape=jax.ShapeDtypeStruct((2 * STEPS + 1,), jnp.int32),
        in_specs=[smem, smem],
        out_specs=smem,
    )(a_index, owners)


def gather_kernel(
    nz, nx, rows, length,
    plan, owners, a_ref, p_ref,
    a_all, p_all,
    xin, src, up, down,
    xin_s, xin_r, up_s, up_r, dn_s, dn_r, xo_s, xo_r, p_s, p_r, own_s,
):
    col = lax.axis_index("col")
    row = lax.axis_index("row")
    z, x = col // nx, col % nx
    slots = a_ref.shape[0] // nx

    barrier = pltpu.get_barrier_semaphore()
    for dz in (1, nz - 1):
        pl.semaphore_signal(
            barrier, inc=1, device_id={"col": (z + dz) % nz * nx + x}, device_id_type=MESH
        )
    for d in range(1, nx):
        pl.semaphore_signal(
            barrier, inc=1, device_id={"col": z * nx + (x + d) % nx}, device_id_type=MESH
        )
    for d in range(1, rows):
        pl.semaphore_signal(barrier, inc=1, device_id={"row": (row + d) % rows}, device_id_type=MESH)
    pl.semaphore_wait(barrier, 2 + nx - 1 + rows - 1)

    def remote(source, target, send, recv, device):
        return pltpu.make_async_remote_copy(
            src_ref=source, dst_ref=target, send_sem=send, recv_sem=recv,
            device_id=device, device_id_type=MESH,
        )

    def xin_copy(d, k):
        return remote(
            a_ref.at[k * nx + (x + d) % nx], xin.at[d - 1, k], xin_s.at[d - 1, k],
            xin_r.at[d - 1, k], {"col": z * nx + (x + d) % nx},
        )

    def up_copy(q):
        return remote(
            up.at[q], up.at[q], up_s.at[q], up_r.at[q], {"col": (z + 1) % nz * nx + x}
        )

    def down_copy(q):
        return remote(
            down.at[q], down.at[q], dn_s.at[q], dn_r.at[q], {"col": (z + nz - 1) % nz * nx + x}
        )

    def xo_copy(d, q, line):
        place = q * nx + line
        return remote(
            a_all.at[place], a_all.at[place], xo_s.at[d - 1, q], xo_r.at[d - 1, q],
            {"col": z * nx + (x + d) % nx},
        )

    def p_copy(d, origin):
        return remote(
            p_ref, p_all.at[origin], p_s.at[d - 1], p_r.at[d - 1], {"row": (row + d) % rows}
        )

    own_p = pltpu.make_async_copy(p_ref, p_all.at[row], own_s)
    starts = [plan[t] for t in range(STEPS)]
    held = [owners[t] for t in range(STEPS)]

    def holder_of(q):
        owner, first = held[0], starts[0]
        for t in range(1, STEPS):
            later = q >= starts[t]
            owner = jnp.where(later, held[t], owner)
            first = jnp.where(later, starts[t], first)
        return owner, jnp.clip(q - first, 0, slots - 1)

    for k in range(slots):
        for d in range(1, nx):
            xin_copy(d, k).start()
    for d in range(1, rows):
        p_copy(d, row).start()
    own_p.start()

    up_lag = z * LAG
    down_lag = (nz - 1 - z) * LAG
    last_lag = jnp.maximum(up_lag, down_lag)

    def step(n, carry):
        @pl.when(n < length)
        def _():
            owner, slot = holder_of(n)
            apart = lax.rem(x + nx - owner % nx, nx)
            value = a_ref[slot * nx + x]

            @pl.when(n < slots)
            def _():
                kept = value
                for d in range(1, nx):
                    xin_copy(d, n).wait_recv()

                    def choose(k, kept, d=d):
                        return pick((apart == d) & (slot == k), xin[d - 1, k], kept)

                    kept = lax.fori_loop(0, n + 1, choose, kept)
                src[n] = kept

            @pl.when(n >= slots)
            def _():
                kept = value
                for d in range(1, nx):
                    kept = pick(apart == d, xin[d - 1, slot], kept)
                src[n] = kept

        q_up = n - up_lag

        @pl.when((q_up >= 0) & (q_up < length))
        def _():
            level = holder_of(q_up)[0] // nx

            @pl.when(z == 0)
            def _():
                up[q_up] = src[q_up]

            @pl.when(z > 0)
            def _():
                up_copy(q_up).wait_recv()
                up[q_up] = pick(level == z, src[q_up], up[q_up])

            @pl.when(z < nz - 1)
            def _():
                up_copy(q_up).start()

        q_down = n - down_lag

        @pl.when((q_down >= 0) & (q_down < length))
        def _():
            level = holder_of(q_down)[0] // nx

            @pl.when(z == nz - 1)
            def _():
                down[q_down] = src[q_down]

            @pl.when(z < nz - 1)
            def _():
                down_copy(q_down).wait_recv()
                down[q_down] = pick(level == z, src[q_down], down[q_down])

            @pl.when(z > 0)
            def _():
                down_copy(q_down).start()

        q = n - last_lag

        @pl.when((q >= 0) & (q < length))
        def _():
            level = holder_of(q)[0] // nx
            a_all[q * nx + x] = pick(level <= z, up[q], down[q])
            for d in range(1, nx):
                xo_copy(d, q, x).start()

        return carry

    lax.fori_loop(0, length + (nz - 1) * LAG, step, 0)

    def finish(q, carry):
        @pl.when(z < nz - 1)
        def _():
            up_copy(q).wait_send()

        @pl.when(z > 0)
        def _():
            down_copy(q).wait_send()

        for d in range(1, nx):
            xo_copy(d, q, x).wait_send()
            xo_copy(d, q, (x + nx - d) % nx).wait_recv()
        return carry

    lax.fori_loop(0, length, finish, 0)
    for k in range(slots):
        for d in range(1, nx):
            xin_copy(d, k).wait_send()
    for d in range(1, rows):
        p_copy(d, row).wait_send()
        p_copy(d, (row + rows - d) % rows).wait_recv()
    own_p.wait()


def gather_live(nz, nx, rows, length, number, plan, owners, a_blocks, p_blocks):
    slots, block = a_blocks.shape[0], a_blocks.shape[1]
    tile = (block // nx, block)
    dma = pltpu.SemaphoreType.DMA
    return pl.pallas_call(
        functools.partial(gather_kernel, nz, nx, rows, length),
        out_shape=(
            jax.ShapeDtypeStruct((length * nx,) + tile, jnp.float32),
            jax.ShapeDtypeStruct((rows,) + p_blocks.shape, jnp.float32),
        ),
        in_specs=[
            pl.BlockSpec(memory_space=pltpu.SMEM),
            pl.BlockSpec(memory_space=pltpu.SMEM),
            pl.BlockSpec(memory_space=pltpu.VMEM),
            pl.BlockSpec(memory_space=pl.ANY),
        ],
        out_specs=(
            pl.BlockSpec(memory_space=pltpu.VMEM),
            pl.BlockSpec(memory_space=pl.ANY),
        ),
        scratch_shapes=[
            pltpu.VMEM((nx - 1, slots) + tile, jnp.float32),
            pltpu.VMEM((length,) + tile, jnp.float32),
            pltpu.VMEM((length,) + tile, jnp.float32),
            pltpu.VMEM((length,) + tile, jnp.float32),
            dma((nx - 1, slots)), dma((nx - 1, slots)),
            dma((length,)), dma((length,)),
            dma((length,)), dma((length,)),
            dma((nx - 1, length)), dma((nx - 1, length)),
            dma((rows - 1,)), dma((rows - 1,)),
            dma,
        ],
        compiler_params=pltpu.CompilerParams(
            collective_id=number, has_side_effects=True, vmem_limit_bytes=40 * 1024 * 1024
        ),
    )(plan, owners, a_blocks.reshape((slots * nx,) + tile), p_blocks)


def split(value):
    high = value.astype(jnp.bfloat16)
    return high, (value - high.astype(jnp.float32)).astype(jnp.bfloat16)


def product_kernel(
    rows, cols, a_slots, width, plan, owners, a_index, p_index, a_all, p_all, out, table
):
    block = a_all.shape[1]
    p_slots = p_all.shape[1]
    row, col = lax.axis_index("row"), lax.axis_index("col")
    out[...] = jnp.zeros_like(out)
    span = width * COL_BLOCKS

    def clear(n, carry):
        table[n] = -1
        return carry

    lax.fori_loop(0, STEPS * span, clear, 0)
    for t in range(STEPS):
        owner = owners[t]
        holder = owner * rows // cols
        offset = owner * width - holder * ROW_BLOCKS
        first = plan[t]
        base = (row * cols + owner) * a_slots

        def place(s, carry):
            entry = p_index[(holder * cols + col) * p_slots + s]
            inner = entry // COL_BLOCKS - offset

            @pl.when((entry >= 0) & (inner >= 0) & (inner < width))
            def _():
                table[t * span + inner * COL_BLOCKS + entry % COL_BLOCKS] = s

            return carry

        lax.fori_loop(0, p_slots, place, 0)

        def one(s, carry):
            entry = a_index[base + s]
            down_rows = entry // width
            inner = entry % width
            for c in range(COL_BLOCKS):
                slot = table[t * span + inner * COL_BLOCKS + c]

                @pl.when(slot >= 0)
                def _():
                    left_high, left_low = split(a_all[first + s])
                    right_high, right_low = split(p_all[holder, slot])
                    dot = functools.partial(jnp.dot, preferred_element_type=jnp.float32)
                    value = dot(left_high, right_high) + (
                        dot(left_high, right_low) + dot(left_low, right_high)
                    )
                    where = pl.ds(pl.multiple_of(down_rows * block, block), block)
                    out[where, c * block : (c + 1) * block] += value

            return carry

        lax.fori_loop(0, plan[STEPS + t], one, 0)


def multiply(rows, cols, a_slots, plan, owners, a_index, p_index, a_all, p_all):
    block = a_all.shape[1]
    width = ROW_BLOCKS * rows // cols
    smem = pl.BlockSpec(memory_space=pltpu.SMEM)
    vmem = pl.BlockSpec(memory_space=pltpu.VMEM)
    return pl.pallas_call(
        functools.partial(product_kernel, rows, cols, a_slots, width),
        out_shape=jax.ShapeDtypeStruct((ROW_BLOCKS * block, COL_BLOCKS * block), jnp.float32),
        in_specs=[smem, smem, smem, smem, vmem, vmem],
        out_specs=vmem,
        scratch_shapes=[pltpu.SMEM((STEPS * width * COL_BLOCKS,), jnp.int32)],
        compiler_params=pltpu.CompilerParams(vmem_limit_bytes=40 * 1024 * 1024),
    )(plan, owners, a_index, p_index, a_all, p_all)


def local(a_blocks, a_index, p_blocks, p_index, owners):
    cols = lax.axis_size("col")
    rows = lax.axis_size("row")
    nz = 4
    nx = cols // nz
    slots = a_blocks.shape[0]
    plan = make_plan(rows, cols, slots, a_index, owners)

    def make(number, length):
        def run(plan, owners, a_blocks, a_index, p_blocks, p_index):
            a_all, p_all = gather_live(
                nz, nx, rows, length, number, plan, owners, a_blocks, p_blocks
            )
            a_all = a_all.reshape((length,) + a_blocks.shape[1:])
            return multiply(rows, cols, slots, plan, owners, a_index, p_index, a_all, p_all)

        return run

    branches = [make(number, length) for number, length in enumerate(LIMITS)]
    return lax.switch(
        plan[2 * STEPS], branches, plan, owners, a_blocks, a_index, p_blocks, p_index
    )


def solution(mesh):
    in_specs = (P(("row", "col"), None, None), P(), P(("row", "col"), None, None), P(), P())
    out_specs = P("row", "col")
    return jax.shard_map(local, mesh=mesh, in_specs=in_specs, out_specs=out_specs, check_vma=False)
```
